32 devices in a mesh: group: 2 (over y), expert: 4 (over z), dp: 4 (over x, core).
Axes of the slice: x: 2, y: 2, z: 4, core: 2. Of those that a mesh axis runs over, the one named last changes fastest.
Arguments:
- out_grad: bfloat16 [1024, 4096], P(('group', 'expert'), 'dp'), parts along dimension 0, may hold values from -6 to 6
- routes: int32 [1024, 8], P(('group', 'expert')), parts along dimension 0, may hold values from 0 to 15, all different within a row; in each aligned block of 128 rows (0 to 127, 128 to 255, ...) at most 128 rows name the same one
- route_prob: float32 [1024, 8], P(('group', 'expert')), parts along dimension 0, may hold values from 0.05 to 1
- down_weight: bfloat16 [16, 768, 4096], P('expert', None, 'dp'), may hold values from -0.21875 to 0.21875
- saved_hidden: bfloat16 [32, 512, 768], P(('group', 'expert'), 'dp'), parts along dimension 0, may hold values from -6 to 6
Outputs:
- scores: float32 [32, 768], P(('group', 'expert')), parts along dimension 0
- down_grad: bfloat16 [32, 768, 4096], P(('group', 'expert'), None, 'dp'), parts along dimension 0
The draws below stay inside these ranges and needn't reach their ends.
There are 2 independent parts, one for each index of `group`. The reference program is written for one: setup_inputs(seed, part) draws one part's arguments, and reference() takes and returns one part's arrays. A program takes and returns all parts, laid end to end along the dimension named above; an argument that names none is the same for every part. Nothing has to cross between parts.
Inputs may be any that keep to these rules, and one draw needn't show every extreme that they name: `routes`: within the 128 tokens of each block no expert is named more than 128 times; each token names 8 different experts.
All inputs are finite; a program needn't handle non-finite values.
Results may differ from the reference program's by a relative error of at most 0.012.
Values may be sent and summed in bfloat16 or wider, within the bound.
No kernel may reach another device: no remote copies, remote signals or barrier semaphores. Data moves between devices by JAX's collectives and lax.ppermute only.
A program may use at most 128 MiB of HBM per device.

```python
import math
import jax
import jax.numpy as jnp
import numpy as np
from jax import lax

D = 4096
FF = 768
TOPK = 8
TOK_DEV = 128
EXPERTS = 16
TOKENS = 512
CAP = 128
SLOTS = 512
N_EXPERT = 4
N_DP = 4


def block_scale(rng, extent, cuts, least, high):
    factor_of = 1.0
    for position, parts in cuts:
        steps = jax.random.uniform(jax.random.fold_in(jax.random.fold_in(rng, 6), position), (parts,), jnp.float32, least / len(cuts), high / len(cuts))
        factor_of = factor_of * jnp.repeat(jnp.exp(steps), extent[position] // parts).reshape((-1,) + (1,) * (len(extent) - 1 - position))
    return factor_of


def assign_block(rng, own, number, rows, count, top, limit, lean):
    sequence = jax.random.permutation(rng, count)
    crowded, common = shares(count, rows * top, limit, lean, True), shares(count, rows * top, limit, lean, False)
    places = jnp.arange(count)

    def named(tallies, turn):
        used = int((tallies > 0).sum())
        fixed = max(1, used // 4)
        shifted = fixed + (places - fixed + turn * (used - fixed)) % max(1, count - fixed)
        return jnp.zeros((count,), jnp.int32).at[sequence[jnp.where(places < fixed, places, shifted)]].set(jnp.asarray(tallies, jnp.int32))

    tallies = jnp.where(number % 4 == 0, named(crowded, number // 4), named(common, number - number // 4 - 1))
    mixed = jax.random.permutation(jax.random.fold_in(own, 3), count)
    giver, sink = mixed[0:count // 2 * 2:2], mixed[1:count // 2 * 2:2]
    slack = jnp.minimum(tallies[giver] - 1, limit - tallies[sink]) // 2
    slack = jnp.where((giver == sequence[0]) | (sink == sequence[0]) | (tallies[sink] == 0), 0, jnp.maximum(slack, 0))
    shifted = jax.random.randint(jax.random.fold_in(own, 4), (count // 2,), 0, 1 << 20) % (slack + 1)
    tallies = tallies.at[giver].add(-shifted).at[sink].add(shifted)
    items = jnp.searchsorted(jnp.cumsum(tallies), jnp.arange(rows * top), side="right").astype(jnp.int32)
    table = items.reshape(top, rows).T
    table = table[jax.random.permutation(jax.random.fold_in(own, 1), rows)]
    turn = jax.random.randint(jax.random.fold_in(own, 2), (rows, 1), 0, top)
    return jnp.take_along_axis(table, (jnp.arange(top)[None, :] + turn) % top, axis=1)


def shares(amount, total, most, skew, full):
    loads = [(1 << 20) // math.isqrt(standing ** skew) + 1 for standing in range(1, amount + 1)]
    largest = most if full else min(most, max(-(-total // amount), total * loads[0] // sum(loads)))
    least = 1 if total - largest >= amount - 1 else 0
    given, surplus = [largest] + [least] * (amount - 1), total - largest - least * (amount - 1)
    while surplus > 0:
        candidates = [i for i in range(1, amount) if given[i] < largest] or [i for i in range(1, amount) if given[i] < most]
        pool, budget = sum([loads[i] for i in candidates]), surplus
        for i in candidates:
            extra = min(most - given[i], max(1, budget * loads[i] // pool), surplus)
            given[i] = given[i] + extra
            surplus = surplus - extra
    return np.array(given)


def gaussian(key, dims, scale, bound, split=(), kind=jnp.bfloat16):
    array = jax.random.normal(key, dims, jnp.float32) * scale
    if len(split) > 0:
        array = block_scale(key, dims, split, -0.22, 0.18) * array
    return jnp.clip(array, min=-bound, max=bound).astype(kind)


def setup_inputs(seed: int = 0, part: int = 0) -> dict:
    arg_keys = jax.random.split(jax.random.key(seed), 6)
    part_splits = jax.random.split(jax.random.fold_in(arg_keys[5], part), 6)
    out_grad = gaussian(part_splits[0], (TOKENS, D), 1.0, 6.0, ((0, 4), (1, 4)))
    routes_keys = jax.random.split(jax.random.fold_in(part_splits[1], 1), TOKENS // TOK_DEV)
    routes_turns = jax.random.permutation(jax.random.fold_in(part_splits[1], 3), TOKENS // TOK_DEV)
    routes = jax.vmap(lambda own, number: assign_block(jax.random.fold_in(part_splits[1], 2), own, number, TOK_DEV, EXPERTS, TOPK, CAP, 2))(routes_keys, routes_turns).reshape((TOKENS, TOPK))
    route_prob = jnp.clip(jnp.exp(math.log(1.0) - 2.9957323 * jax.random.uniform(part_splits[2], (TOKENS, TOPK), jnp.float32) ** block_scale(part_splits[2], (TOKENS, TOPK), ((0, 4),), -0.2, 0.2)), 0.05, 1.0)
    down_weight = gaussian(arg_keys[3], (EXPERTS, FF, D), FF ** -0.5, 0.21875, ((0, 4), (2, 4)))
    saved_hidden = gaussian(part_splits[4], (EXPERTS, SLOTS, FF), 1.0, 6.0, ((0, 4), (1, 4)))
    return dict(out_grad=out_grad, routes=routes, route_prob=route_prob, down_weight=down_weight, saved_hidden=saved_hidden)


def reference(out_grad, routes, route_prob, down_weight, saved_hidden):
    slot_total = N_EXPERT * CAP
    flat_routes = routes.reshape(N_EXPERT, TOK_DEV * TOPK)
    one_hot = (flat_routes[:, :, None] == jnp.arange(EXPERTS, dtype=jnp.int32)[None, None, :]).astype(jnp.int32)
    slot_rank = jnp.sum((jnp.cumsum(one_hot, axis=1) - 1) * one_hot, axis=2)
    slot_index = (jnp.arange(N_EXPERT, dtype=jnp.int32)[:, None] * CAP + slot_rank).reshape(-1).astype(jnp.int32)
    token_index = (jnp.arange(TOKENS * TOPK, dtype=jnp.int32) // TOPK).astype(jnp.int32)
    expert_index = routes.reshape(-1).astype(jnp.int32)
    token_table = jnp.zeros((EXPERTS, slot_total), jnp.int32).at[expert_index, slot_index].set(token_index)
    weight_table = jnp.zeros((EXPERTS, slot_total), jnp.float32).at[expert_index, slot_index].set(route_prob.reshape(-1))

    def one_expert(inputs):
        tokens_of, weights_of, weight_down, hidden_saved = inputs
        routed = (out_grad[tokens_of].astype(jnp.float32) * weights_of[:, None]).astype(jnp.bfloat16)
        blocks = routed.astype(jnp.float32).reshape(slot_total, N_DP, D // N_DP)
        weight_blocks = weight_down.astype(jnp.float32).reshape(FF, N_DP, D // N_DP)
        partial_value = jnp.einsum("snc,fnc->nsf", blocks, weight_blocks)
        partial_value = lax.optimization_barrier(partial_value.astype(jnp.bfloat16)).astype(jnp.float32)
        hidden_grad = jnp.sum(partial_value, axis=0)
        neuron_scores = jnp.sum((hidden_saved.astype(jnp.float32) * hidden_grad) ** 2, axis=0)
        gradient = jnp.dot(hidden_saved.T, routed, preferred_element_type=jnp.float32).astype(jnp.bfloat16)
        return neuron_scores, gradient

    scores, down_grad = lax.map(one_expert, (token_table, weight_table, down_weight, saved_hidden))
    return scores, down_grad
```

```python
import functools

import jax
import jax.numpy as jnp
from jax import lax
from jax.experimental import pallas as pl
from jax.experimental.pallas import tpu as pltpu
from jax.sharding import PartitionSpec as P

CORES = 2


def rotate(value, axis, step):
    count = lax.axis_size(axis)
    return lax.ppermute(value, axis, [(i, (i + step) % count) for i in range(count)])


def dp_shift(value, chip_step, core_flip):
    count = lax.axis_size("dp")
    chips = count // CORES
    pairs = []
    for chip in range(chips):
        for core in range(CORES):
            target = (chip - chip_step) % chips
            pairs.append((chip * CORES + core, target * CORES + (core ^ core_flip)))
    return lax.ppermute(value, "dp", pairs)


def ring_gather(block):
    owners = lax.axis_size("expert")
    rows = block.shape[0]
    got = {0: [block]}
    ahead = behind = block
    for step in range(1, owners // 2):
        behind = rotate(behind, "expert", 1)
        ahead = rotate(ahead, "expert", -1)
        got[owners - step] = [behind]
        got[step] = [ahead]
    half = rows // 2
    top = rotate(ahead[:half], "expert", -1)
    low = rotate(behind[half:], "expert", 1)
    got[owners // 2] = [top, low]
    return [got[r] for r in range(owners)]


def dispatch_body(pieces, first, order, routes, probs, *refs):
    total = sum(pieces)
    blocks, (weight, routed, keep, send, table) = refs[:total], refs[total:]
    owners, capacity = routes.shape[0], routed.shape[1] // routes.shape[0]
    tokens = routes.shape[2]

    at = 0
    for r, count in enumerate(pieces):
        row = 0
        for _ in range(count):
            part = blocks[at]
            table[r, row : row + part.shape[0], :] = part[...]
            row += part.shape[0]
            at += 1

    expert = order[owners] + first + pl.program_id(0)
    named, weights = [], []
    for r in range(owners):
        hit = routes[r] == expert
        named.append(jnp.max(hit.astype(jnp.float32), axis=0, keepdims=True))
        weights.append(jnp.sum(jnp.where(hit, probs[r], 0.0), axis=0, keepdims=True))
    named = jnp.concatenate(named, axis=0)
    before = (
        lax.broadcasted_iota(jnp.int32, (tokens, tokens), 0)
        < lax.broadcasted_iota(jnp.int32, (tokens, tokens), 1)
    )
    rank = jnp.dot(
        named.astype(jnp.bfloat16),
        before.astype(jnp.float32).astype(jnp.bfloat16),
        preferred_element_type=jnp.float32,
    )
    place = jnp.where(named > 0.0, rank, -1.0).astype(jnp.int32)
    slots = lax.broadcasted_iota(jnp.int32, (capacity, tokens), 0)
    for r in range(owners):
        taken = slots == place[r : r + 1, :]
        rows = jnp.dot(
            taken.astype(jnp.float32).astype(jnp.bfloat16),
            table[r],
            preferred_element_type=jnp.float32,
        )
        scale = jnp.sum(jnp.where(taken, weights[r], 0.0), axis=1, keepdims=True)
        position = pl.multiple_of(order[r] * capacity, capacity)
        routed[0, pl.ds(position, capacity), :] = (rows * scale).astype(jnp.bfloat16)
    partial_value = lax.dot_general(
        routed[0], weight[0], (((1,), (1,)), ((), ())), preferred_element_type=jnp.float32
    ).astype(jnp.bfloat16)
    half = partial_value.shape[0] // CORES
    keep[0] = partial_value[:half]
    send[0] = partial_value[half:]


def dispatch(order, routes, probs, blocks, down_weight, first, count, capacity):
    owners, fanout, tokens = routes.shape
    _, hidden, columns = down_weight.shape
    slots = owners * capacity
    flat = [part for parts in blocks for part in parts]
    whole = lambda shape: pl.BlockSpec(shape, lambda e, order: (0,) * len(shape))
    by_expert = lambda shape: pl.BlockSpec((1,) + shape, lambda e, order: (e, 0, 0))
    return pl.pallas_call(
        functools.partial(dispatch_body, [len(parts) for parts in blocks], first),
        grid_spec=pltpu.PrefetchScalarGridSpec(
            num_scalar_prefetch=1,
            grid=(count,),
            in_specs=[whole(routes.shape), whole(probs.shape)]
            + [whole(part.shape) for part in flat]
            + [pl.BlockSpec((1, hidden, columns), lambda e, order: (first + e, 0, 0))],
            out_specs=[
                by_expert((slots, columns)),
                by_expert((slots // CORES, hidden)),
                by_expert((slots // CORES, hidden)),
            ],
            scratch_shapes=[pltpu.VMEM((owners, tokens, columns), jnp.bfloat16)],
        ),
        out_shape=[
            jax.ShapeDtypeStruct((count, slots, columns), jnp.bfloat16),
            jax.ShapeDtypeStruct((count, slots // CORES, hidden), jnp.bfloat16),
            jax.ShapeDtypeStruct((count, slots // CORES, hidden), jnp.bfloat16),
        ],
        compiler_params=pltpu.CompilerParams(vmem_limit_bytes=40 * 2**20),
        cost_estimate=pl.CostEstimate(
            flops=2 * count * slots * columns * (hidden + tokens),
            bytes_accessed=2 * count * (hidden * columns + slots * (columns + hidden)),
            transcendentals=0,
        ),
    )(order, routes, probs, *flat, down_weight)


def gradient_body(*refs):
    saved, (routed, out) = refs[:-2], refs[-2:]
    whole = jnp.concatenate([part[0] for part in saved], axis=0)
    out[0] = lax.dot_general(
        whole, routed[0], (((0,), (0,)), ((), ())), preferred_element_type=jnp.float32
    ).astype(jnp.bfloat16)


def gradient_of(saved, routed):
    experts, slots, columns = routed.shape
    hidden = saved[0].shape[2]
    by_expert = lambda shape: pl.BlockSpec((1,) + shape, lambda e: (e, 0, 0))
    return pl.pallas_call(
        gradient_body,
        grid=(experts,),
        in_specs=[by_expert(part.shape[1:]) for part in saved] + [by_expert((slots, columns))],
        out_specs=by_expert((hidden, columns)),
        out_shape=jax.ShapeDtypeStruct((experts, hidden, columns), jnp.bfloat16),
        compiler_params=pltpu.CompilerParams(vmem_limit_bytes=40 * 2**20),
        cost_estimate=pl.CostEstimate(
            flops=2 * experts * slots * columns * hidden,
            bytes_accessed=2 * experts * (hidden * columns + slots * (columns + hidden)),
            transcendentals=0,
        ),
    )(*saved, routed)


def shards(out_grad, routes, route_prob, down_weight, saved_hidden):
    owners = lax.axis_size("expert")
    dp_count = lax.axis_size("dp")
    chips = dp_count // CORES
    local_experts, share_rows, _ = saved_hidden.shape
    capacity = share_rows * dp_count // owners
    assert capacity == share_rows
    mine, index = lax.axis_index("expert"), lax.axis_index("dp")
    chip, core = index // CORES, index % CORES

    source = (mine + jnp.arange(owners, dtype=jnp.int32)) % owners
    position = (source % CORES != core) * chips + (source // CORES - chip) % chips
    order = jnp.concatenate([position, (mine * local_experts)[None]]).astype(jnp.int32)

    saved = [saved_hidden]
    for step in range(1, chips):
        saved.append(dp_shift(saved_hidden, step, 0))
    saved = saved + [dp_shift(part, 0, 1) for part in saved]

    route_rows = [routes.T] + [rotate(routes.T, "expert", -r) for r in range(1, owners)]
    prob_rows = [route_prob.T] + [rotate(route_prob.T, "expert", -r) for r in range(1, owners)]
    route_rows, prob_rows = jnp.stack(route_rows), jnp.stack(prob_rows)
    blocks = ring_gather(out_grad)

    routed, squares = [], []
    for e in range(local_experts):
        rows, keep, send = dispatch(
            order, route_rows, prob_rows, blocks, down_weight, e, 1, capacity
        )
        routed.append(rows)
        other = dp_shift(send, 0, 1)
        total = keep.astype(jnp.float32) + other.astype(jnp.float32)
        hidden_grad = total[0, :share_rows]
        for step in range(1, chips):
            leaving = total[0, step * share_rows : (step + 1) * share_rows].astype(jnp.bfloat16)
            hidden_grad = hidden_grad + dp_shift(leaving, -step, 0).astype(jnp.float32)
        squares.append(jnp.sum((saved_hidden[e].astype(jnp.float32) * hidden_grad) ** 2, axis=0))
    local = jnp.stack(squares)
    local = local + dp_shift(local, 0, 1)
    parts = [local] + [dp_shift(local, step, 0) for step in range(1, chips)]
    if chips > 2:
        parts = jnp.roll(jnp.stack(parts), chip, axis=0)
        scores = jnp.sum(parts, axis=0)
    else:
        scores = sum(parts)

    gradient = gradient_of(saved, jnp.concatenate(routed, axis=0))
    return (scores, gradient)


def solution(mesh):
    placed = (
        P(("group", "expert"), "dp"),
        P(("group", "expert"), None),
        P(("group", "expert"), None),
        P("expert", None, "dp"),
        P(("group", "expert"), "dp", None),
    )
    return jax.shard_map(
        shards,
        mesh=mesh,
        in_specs=placed,
        out_specs=(P(("group", "expert"), None), P(("group", "expert"), None, "dp")),
        check_vma=False,
    )
```

```python
import functools

import jax
import jax.numpy as jnp
from jax import lax
from jax.experimental import pallas as pl
from jax.experimental.pallas import tpu as pltpu
from jax.sharding import PartitionSpec as P

CORES = 2
ROWS = 16
VMEM_LIMIT = 24 * 2**20
VMEM = pl.BlockSpec(memory_space=pltpu.VMEM)
HBM = pl.BlockSpec(memory_space=pltpu.HBM)


def exchange(value, step):
    count = lax.axis_size("expert")
    return lax.ppermute(value, "expert", [(i, i ^ step) for i in range(count)])


def dp_shift(value, chip_step, core_flip):
    chips = lax.axis_size("dp") // CORES
    pairs = []
    for chip in range(chips):
        for core in range(CORES):
            target = (chip - chip_step) % chips
            pairs.append((chip * CORES + core, target * CORES + (core ^ core_flip)))
    return lax.ppermute(value, "dp", pairs)


def pack(out_grad, routes, route_prob):
    tokens, columns = out_grad.shape
    assert 2 * tokens <= columns and 2 * routes.shape[1] == ROWS
    value = route_prob.T
    high = lax.reduce_precision(value, 8, 7)
    middle = lax.reduce_precision(value - high, 8, 7)
    upper = jnp.concatenate([routes.T.astype(jnp.float32), high], axis=1)
    lower = jnp.concatenate([middle, value - high - middle], axis=1)
    known = jnp.concatenate([upper, lower], axis=0).astype(jnp.bfloat16)
    known = jnp.pad(known, ((0, 0), (0, columns - known.shape[1])))
    return jnp.concatenate([out_grad, known], axis=0)


def saved_at(block, chips):
    index = lax.axis_index("dp")
    chip, core = index // CORES, index % CORES
    return (block % CORES != core) * chips + (block // CORES - chip + chips) % chips


def phase_body(group, parts, *refs):
    blocks, weight = refs[:group], refs[group]
    routed, keep, send, made = refs[-4:]
    experts, rows, columns = routed.shape
    chips = keep.shape[0]
    capacity, share = rows // group, rows // parts
    tokens, fanout = blocks[0].shape[0] - ROWS, ROWS // 2
    mine, index = lax.axis_index("expert"), lax.axis_index("dp")
    chip, core = index // CORES, index % CORES

    before = (
        lax.broadcasted_iota(jnp.int32, (tokens, tokens), 0)
        < lax.broadcasted_iota(jnp.int32, (tokens, tokens), 1)
    )
    before = before.astype(jnp.float32).astype(jnp.bfloat16)
    slots = lax.broadcasted_iota(jnp.int32, (capacity, tokens), 0)
    for g in range(group):
        known = blocks[g][tokens:, : 2 * tokens].astype(jnp.float32)
        names = known[:fanout, :tokens]
        probs = known[:fanout, tokens:] + known[fanout:, :tokens] + known[fanout:, tokens:]
        named, weights = [], []
        for e in range(experts):
            hit = names == (mine * experts + e).astype(jnp.float32)
            prob = jnp.where(hit, probs, 0.0)
            named.append(jnp.max(hit.astype(jnp.float32), axis=0, keepdims=True))
            weights.append(jnp.sum(prob, axis=0, keepdims=True))
        named = jnp.concatenate(named, axis=0)
        rank = jnp.dot(named.astype(jnp.bfloat16), before, preferred_element_type=jnp.float32)
        place = jnp.where(named > 0.0, rank, -1.0).astype(jnp.int32)
        for e in range(experts):
            taken = slots == place[e : e + 1, :]
            chosen = jnp.dot(
                taken.astype(jnp.float32).astype(jnp.bfloat16),
                blocks[g][:tokens],
                preferred_element_type=jnp.float32,
            )
            scale = jnp.sum(jnp.where(taken, weights[e], 0.0), axis=1, keepdims=True)
            routed[e, g * capacity : (g + 1) * capacity, :] = (chosen * scale).astype(jnp.bfloat16)
    for e in range(experts):
        value = lax.dot_general(
            weight[e], routed[e], (((1,), (1,)), ((), ())), preferred_element_type=jnp.float32
        )
        value = value.T.astype(jnp.bfloat16)
        for p in range(parts):
            made[e * parts + p] = value[p * share : (p + 1) * share]
    for k in range(chips):
        near = (chip + k) % chips * CORES
        keep[k] = made[near + core]
        send[k] = made[near + 1 - core]


def phase(blocks, down_weight, capacity, parts, after):
    experts, hidden, columns = down_weight.shape
    group = len(blocks)
    rows = group * capacity
    chips = experts * parts // CORES
    half = jax.ShapeDtypeStruct((chips, rows // parts, hidden), jnp.bfloat16)
    return pl.pallas_call(
        functools.partial(phase_body, group, parts),
        in_specs=[VMEM] * (group + 1) + [HBM] * len(after),
        out_specs=[VMEM] * 3,
        out_shape=[jax.ShapeDtypeStruct((experts, rows, columns), jnp.bfloat16), half, half],
        scratch_shapes=[pltpu.VMEM((experts * parts, rows // parts, hidden), jnp.bfloat16)],
        compiler_params=pltpu.CompilerParams(vmem_limit_bytes=VMEM_LIMIT),
        cost_estimate=pl.CostEstimate(
            flops=2 * experts * rows * columns * hidden,
            bytes_accessed=2 * experts * hidden * columns,
            transcendentals=0,
        ),
    )(*blocks, down_weight, *after)


def score_body(phases, pieces, group, parts, *refs):
    out, table = refs[-2:]
    spread, capacity, _ = table.shape
    saved, hidden = refs[:spread], refs[spread : spread + pieces]
    per = len(hidden) // phases
    chips = spread // CORES
    mine, index = lax.axis_index("expert"), lax.axis_index("dp")
    expert = index // parts
    row = index % parts * hidden[0].shape[0]
    for i in range(spread):
        table[i] = saved[i][expert]
    total = jnp.zeros((1, out.shape[1]), jnp.float32)
    for j in range(phases):
        grad = hidden[j * per][...]
        for more in hidden[j * per + 1 : (j + 1) * per]:
            grad = grad + more[...].astype(jnp.float32)
        at = saved_at(mine ^ (j * group + row // capacity), chips)
        offset = pl.multiple_of(row % capacity, ROWS)
        kept = table[at, pl.ds(offset, grad.shape[0]), :].astype(jnp.float32)
        total = total + jnp.sum((kept * grad) ** 2, axis=0, keepdims=True)
    line = lax.broadcasted_iota(jnp.int32, out.shape, 0)
    out[...] = jnp.where(line == expert, total, 0.0)


def score(saved, hidden, group, parts, after):
    experts, share, width = saved[0].shape
    flat = [piece for pieces in hidden for piece in pieces]
    return pl.pallas_call(
        functools.partial(score_body, len(hidden), len(flat), group, parts),
        in_specs=[VMEM] * (len(saved) + len(flat)) + [HBM] * len(after),
        out_specs=VMEM,
        out_shape=jax.ShapeDtypeStruct((experts, width), jnp.float32),
        scratch_shapes=[pltpu.VMEM((len(saved), share, width), jnp.bfloat16)],
        compiler_params=pltpu.CompilerParams(vmem_limit_bytes=VMEM_LIMIT),
    )(*saved, *flat, *after)


def gradient_body(spread, *refs):
    saved, routed = refs[:spread], refs[spread:-3]
    out, done, rows = refs[-3:]
    done[...] = jnp.zeros_like(done)
    e = pl.program_id(0)
    share = saved[0].shape[1]
    mine, index = lax.axis_index("expert"), lax.axis_index("dp")
    chips = spread // CORES
    for i in range(spread):
        near = (index // CORES + i % chips) % chips * CORES
        block = near + (index % CORES if i < chips else 1 - index % CORES)
        at = pl.multiple_of((block ^ mine) * share, share)
        rows[pl.ds(at, share), :] = saved[i][e]
    whole = jnp.concatenate([part[e] for part in routed], axis=0)
    out[0] = lax.dot_general(
        rows[...], whole, (((0,), (0,)), ((), ())), preferred_element_type=jnp.float32
    ).astype(jnp.bfloat16)


def gradient_of(saved, routed):
    experts, share, hidden = saved[0].shape
    columns = routed[0].shape[2]
    slots = share * len(saved)
    return pl.pallas_call(
        functools.partial(gradient_body, len(saved)),
        grid=(experts,),
        in_specs=[VMEM] * (len(saved) + len(routed)),
        out_specs=[
            pl.BlockSpec((1, hidden, columns), lambda e: (e, 0, 0)),
            pl.BlockSpec((8, 128), lambda e: (0, 0)),
        ],
        out_shape=[
            jax.ShapeDtypeStruct((experts, hidden, columns), jnp.bfloat16),
            jax.ShapeDtypeStruct((8, 128), jnp.float32),
        ],
        scratch_shapes=[pltpu.VMEM((slots, hidden), jnp.bfloat16)],
        compiler_params=pltpu.CompilerParams(vmem_limit_bytes=VMEM_LIMIT),
        cost_estimate=pl.CostEstimate(
            flops=2 * experts * slots * columns * hidden,
            bytes_accessed=2 * experts * hidden * columns,
            transcendentals=0,
        ),
    )(*saved, *routed)


def shards(out_grad, routes, route_prob, down_weight, saved_hidden):
    owners = lax.axis_size("expert")
    dp_count = lax.axis_size("dp")
    chips = dp_count // CORES
    experts, capacity, _ = saved_hidden.shape
    assert owners == dp_count and dp_count % experts == 0
    parts = dp_count // experts
    group = max(1, parts * ROWS // capacity)
    phases = owners // group
    index = lax.axis_index("dp")

    packed = pack(out_grad, routes, route_prob)
    blocks = [packed] + [exchange(packed, j) for j in range(1, owners)]

    saved = [saved_hidden] + [dp_shift(saved_hidden, step, 0) for step in range(1, chips)]

    order = [0, 1, 3, 2] if phases == 4 else list(range(phases))
    routed, hidden = [None] * phases, [None] * phases
    for j in order:
        routed[j], keep, send = phase(
            blocks[j * group : (j + 1) * group],
            down_weight,
            capacity,
            parts,
            [],
        )
        other = dp_shift(send, 0, 1)
        total = keep.astype(jnp.float32) + other.astype(jnp.float32)
        hidden[j] = [total[0]] + [
            dp_shift(total[step].astype(jnp.bfloat16), -step, 0) for step in range(1, chips)
        ]
    saved = saved + [dp_shift(part, 0, 1) for part in saved]
    gradient, done = gradient_of(saved, routed)
    local = score(saved, hidden, group, parts, [done])
    pieces = [
        dp_shift(local, step, flip)
        for step in range(chips)
        for flip in range(CORES)
        if step + flip
    ]
    if parts > 1:
        pieces = jnp.stack([local] + pieces).reshape(chips, CORES, experts, -1)
        pieces = jnp.where(index % CORES == 0, pieces, pieces[:, ::-1])
        scores = jnp.sum(jnp.roll(pieces, index // CORES, axis=0), axis=(0, 1))
    else:
        scores = sum(pieces, local)
    return (scores, gradient)


def solution(mesh):
    placed = (
        P(("group", "expert"), "dp"),
        P(("group", "expert"), None),
        P(("group", "expert"), None),
        P("expert", None, "dp"),
        P(("group", "expert"), "dp", None),
    )
    return jax.shard_map(
        shards,
        mesh=mesh,
        in_specs=placed,
        out_specs=(P(("group", "expert"), None), P(("group", "expert"), None, "dp")),
        check_vma=False,
    )
```

```python
import functools

import jax
import jax.numpy as jnp
from jax import lax
from jax.experimental import pallas as pl
from jax.experimental.pallas import tpu as pltpu
from jax.sharding import PartitionSpec as P

CORES = 2
ROWS = 16
VMEM_LIMIT = 14 * 2**20
VMEM = pl.BlockSpec(memory_space=pltpu.VMEM)
ANY = pl.BlockSpec(memory_space=pl.ANY)


def exchange(value, step):
    count = lax.axis_size("expert")
    return lax.ppermute(value, "expert", [(i, i ^ step) for i in range(count)])


def look_up(table, index):
    return sum(jnp.where(index == i, int(value), 0) for i, value in enumerate(table))


def gather_plan(packed):
    owners = lax.axis_size("expert")
    mine = lax.axis_index("expert")
    own = ([packed], [0] * owners, list(range(owners)))
    if owners != 4:
        return [own] + [
            ([exchange(packed, j)], [0] * owners, [i ^ j for i in range(owners)])
            for j in range(1, owners)
        ]
    send = lambda value, pairs: lax.ppermute(value, "expert", pairs)
    down = send(packed, [(1, 0), (2, 1), (3, 2)])
    up = send(packed, [(0, 1), (1, 2), (2, 3)])
    far = send(packed, [(0, 2), (3, 1)])
    outer = [(1, 0), (2, 3)]
    second = send(jnp.where(mine == 1, down, up), outer)
    third = send(far, outer)
    return [
        own,
        ([down, up], [0, 0, 0, 1], [1, 2, 3, 2]),
        ([second, up], [0, 1, 1, 0], [2, 0, 1, 1]),
        ([third, far], [0, 1, 1, 0], [3, 3, 0, 0]),
    ]


def dp_shift(value, chip_step, core_flip):
    chips = lax.axis_size("dp") // CORES
    pairs = []
    for chip in range(chips):
        for core in range(CORES):
            target = (chip - chip_step) % chips
            pairs.append((chip * CORES + core, target * CORES + (core ^ core_flip)))
    return lax.ppermute(value, "dp", pairs)


def pack(out_grad, routes, route_prob):
    tokens, columns = out_grad.shape
    assert 2 * tokens <= columns and 2 * routes.shape[1] == ROWS
    value = route_prob.T
    high = lax.reduce_precision(value, 8, 7)
    middle = lax.reduce_precision(value - high, 8, 7)
    upper = jnp.concatenate([routes.T.astype(jnp.float32), high], axis=1)
    lower = jnp.concatenate([middle, value - high - middle], axis=1)
    known = jnp.concatenate([upper, lower], axis=0).astype(jnp.bfloat16)
    known = jnp.pad(known, ((0, 0), (0, columns - known.shape[1])))
    return jnp.concatenate([out_grad, known], axis=0)


def saved_at(block, chips):
    index = lax.axis_index("dp")
    chip, core = index // CORES, index % CORES
    return (block % CORES != core) * chips + (block // CORES - chip + chips) % chips


def phase_body(picks, arrays, parts, *refs):
    group = len(picks)
    choices, weight = refs[: sum(arrays)], refs[sum(arrays)]
    routed, keep, send, made, table = refs[-5:]
    experts, rows, columns = routed.shape
    chips = keep.shape[0]
    capacity, share = rows // group, rows // parts
    tokens, fanout = choices[0].shape[0] - ROWS, ROWS // 2
    mine, index = lax.axis_index("expert"), lax.axis_index("dp")
    chip, core = index // CORES, index % CORES

    before = (
        lax.broadcasted_iota(jnp.int32, (tokens, tokens), 0)
        < lax.broadcasted_iota(jnp.int32, (tokens, tokens), 1)
    )
    before = before.astype(jnp.float32).astype(jnp.bfloat16)
    slots = lax.broadcasted_iota(jnp.int32, (capacity, tokens), 0)
    blocks, at = [], 0
    for g in range(group):
        options = choices[at : at + arrays[g]]
        at += arrays[g]
        if len(options) == 1:
            blocks.append(options[0])
            continue
        pick = look_up(picks[g], mine)
        for i, option in enumerate(options):

            @pl.when(pick == i)
            def _(option=option, g=g):
                table[g] = option[...]

        blocks.append(table.at[g])
    for g in range(group):
        known = blocks[g][tokens:, : 2 * tokens].astype(jnp.float32)
        names = known[:fanout, :tokens]
        probs = known[:fanout, tokens:] + known[fanout:, :tokens] + known[fanout:, tokens:]
        named, weights = [], []
        for e in range(experts):
            hit = names == (mine * experts + e).astype(jnp.float32)
            prob = jnp.where(hit, probs, 0.0)
            named.append(jnp.max(hit.astype(jnp.float32), axis=0, keepdims=True))
            weights.append(jnp.sum(prob, axis=0, keepdims=True))
        named = jnp.concatenate(named, axis=0)
        rank = jnp.dot(named.astype(jnp.bfloat16), before, preferred_element_type=jnp.float32)
        place = jnp.where(named > 0.0, rank, -1.0).astype(jnp.int32)
        for e in range(experts):
            taken = slots == place[e : e + 1, :]
            chosen = jnp.dot(
                taken.astype(jnp.float32).astype(jnp.bfloat16),
                blocks[g][:tokens],
                preferred_element_type=jnp.float32,
            )
            scale = jnp.sum(jnp.where(taken, weights[e], 0.0), axis=1, keepdims=True)
            routed[e, g * capacity : (g + 1) * capacity, :] = (chosen * scale).astype(jnp.bfloat16)
    for e in range(experts):
        value = lax.dot_general(
            weight[e], routed[e], (((1,), (1,)), ((), ())), preferred_element_type=jnp.float32
        )
        value = value.T.astype(jnp.bfloat16)
        for p in range(parts):
            made[e * parts + p] = value[p * share : (p + 1) * share]
    for k in range(chips):
        near = (chip + k) % chips * CORES
        keep[k] = made[near + core]
        send[k] = made[near + 1 - core]


def phase(blocks, down_weight, capacity, parts, after):
    experts, hidden, columns = down_weight.shape
    group = len(blocks)
    arrays = [len(options) for options, _, _ in blocks]
    flat = [array for options, _, _ in blocks for array in options]
    rows = group * capacity
    chips = experts * parts // CORES
    half = jax.ShapeDtypeStruct((chips, rows // parts, hidden), jnp.bfloat16)
    return pl.pallas_call(
        functools.partial(phase_body, [pick for _, pick, _ in blocks], arrays, parts),
        in_specs=[VMEM] * (len(flat) + 1) + [ANY] * len(after),
        out_specs=[VMEM] * 3,
        out_shape=[jax.ShapeDtypeStruct((experts, rows, columns), jnp.bfloat16), half, half],
        scratch_shapes=[
            pltpu.VMEM((experts * parts, rows // parts, hidden), jnp.bfloat16),
            pltpu.VMEM((group,) + flat[0].shape, jnp.bfloat16),
        ],
        compiler_params=pltpu.CompilerParams(vmem_limit_bytes=VMEM_LIMIT),
        cost_estimate=pl.CostEstimate(
            flops=5 * experts * rows * columns * hidden,
            bytes_accessed=5 * experts * hidden * columns,
            transcendentals=0,
        ),
    )(*flat, down_weight, *after)


def score_body(tables, pieces, parts, *refs):
    out, table = refs[-2:]
    spread, capacity, _ = table.shape
    saved, hidden = refs[:spread], refs[spread : spread + pieces]
    phases = pieces * CORES // spread
    group, per = len(tables) // phases, spread // CORES
    chips = spread // CORES
    mine, index = lax.axis_index("expert"), lax.axis_index("dp")
    expert = index // parts
    row = index % parts * hidden[0].shape[0]
    for i in range(spread):
        table[i] = saved[i][expert]
    total = jnp.zeros((1, out.shape[1]), jnp.float32)
    for j in range(phases):
        grad = hidden[j * per][...]
        for more in hidden[j * per + 1 : (j + 1) * per]:
            grad = grad + more[...].astype(jnp.float32)
        block = sum(
            jnp.where(row // capacity == g, look_up(tables[j * group + g], mine), 0)
            for g in range(group)
        )
        at = saved_at(block, chips)
        offset = pl.multiple_of(row % capacity, ROWS)
        kept = table[at, pl.ds(offset, grad.shape[0]), :].astype(jnp.float32)
        total = total + jnp.sum((kept * grad) ** 2, axis=0, keepdims=True)
    line = lax.broadcasted_iota(jnp.int32, out.shape, 0)
    out[...] = jnp.where(line == expert, total, 0.0)


def score(saved, hidden, tables, parts, after):
    experts, share, width = saved[0].shape
    flat = [piece for pieces in hidden for piece in pieces]
    return pl.pallas_call(
        functools.partial(score_body, tables, len(flat), parts),
        in_specs=[VMEM] * (len(saved) + len(flat)) + [ANY] * len(after),
        out_specs=VMEM,
        out_shape=jax.ShapeDtypeStruct((experts, width), jnp.float32),
        scratch_shapes=[pltpu.VMEM((len(saved), share, width), jnp.bfloat16)],
        compiler_params=pltpu.CompilerParams(vmem_limit_bytes=VMEM_LIMIT),
    )(*saved, *flat, *after)


def gradient_body(spread, tables, *refs):
    saved, routed = refs[:spread], refs[spread:-3]
    out, done, rows = refs[-3:]
    done[...] = jnp.zeros_like(done)
    e = pl.program_id(0)
    share = saved[0].shape[1]
    mine, index = lax.axis_index("expert"), lax.axis_index("dp")
    chips = spread // CORES
    for i in range(spread):
        near = (index // CORES + i % chips) % chips * CORES
        block = near + (index % CORES if i < chips else 1 - index % CORES)
        order = sum(
            jnp.where(look_up(table, mine) == block, j, 0) for j, table in enumerate(tables)
        )
        at = pl.multiple_of(order * share, share)
        rows[pl.ds(at, share), :] = saved[i][e]
    whole = jnp.concatenate([part[e] for part in routed], axis=0)
    out[0] = lax.dot_general(
        rows[...], whole, (((0,), (0,)), ((), ())), preferred_element_type=jnp.float32
    ).astype(jnp.bfloat16)


def gradient_of(saved, routed, tables):
    experts, share, hidden = saved[0].shape
    columns = routed[0].shape[2]
    slots = share * len(saved)
    return pl.pallas_call(
        functools.partial(gradient_body, len(saved), tables),
        grid=(experts,),
        in_specs=[VMEM] * (len(saved) + len(routed)),
        out_specs=[
            pl.BlockSpec((1, hidden, columns), lambda e: (e, 0, 0)),
            pl.BlockSpec((8, 128), lambda e: (0, 0)),
        ],
        out_shape=[
            jax.ShapeDtypeStruct((experts, hidden, columns), jnp.bfloat16),
            jax.ShapeDtypeStruct((8, 128), jnp.float32),
        ],
        scratch_shapes=[pltpu.VMEM((slots, hidden), jnp.bfloat16)],
        compiler_params=pltpu.CompilerParams(vmem_limit_bytes=VMEM_LIMIT),
        cost_estimate=pl.CostEstimate(
            flops=5 * experts * slots * columns * hidden,
            bytes_accessed=5 * experts * hidden * columns,
            transcendentals=0,
        ),
    )(*saved, *routed)


def shards(out_grad, routes, route_prob, down_weight, saved_hidden):
    owners = lax.axis_size("expert")
    dp_count = lax.axis_size("dp")
    chips = dp_count // CORES
    experts, capacity, _ = saved_hidden.shape
    assert owners == dp_count and dp_count % experts == 0
    parts = dp_count // experts
    group = max(1, parts * ROWS // capacity)
    phases = owners // group
    index = lax.axis_index("dp")

    packed = pack(out_grad, routes, route_prob)
    plan = gather_plan(packed)
    tables = [table for _, _, table in plan]

    saved = [saved_hidden] + [dp_shift(saved_hidden, step, 0) for step in range(1, chips)]

    routed, hidden = [None] * phases, [None] * phases
    for j in range(phases):
        routed[j], keep, send = phase(
            plan[j * group : (j + 1) * group],
            down_weight,
            capacity,
            parts,
            hidden[0][:1] if j == 2 else hidden[0][1:] + hidden[1][:1] if j == 3 else [],
        )
        other = dp_shift(send, 0, 1)
        total = keep.astype(jnp.float32) + other.astype(jnp.float32)
        hidden[j] = [total[0]] + [
            dp_shift(total[step].astype(jnp.bfloat16), -step, 0) for step in range(1, chips)
        ]
    saved = saved + [dp_shift(part, 0, 1) for part in saved]
    gradient, done = gradient_of(saved, routed, tables)
    local = score(saved, hidden, tables, parts, [done])
    pieces = [
        dp_shift(local, step, flip)
        for step in range(chips)
        for flip in range(CORES)
        if step + flip
    ]
    if parts > 1:
        pieces = jnp.stack([local] + pieces).reshape(chips, CORES, experts, -1)
        pieces = jnp.where(index % CORES == 0, pieces, pieces[:, ::-1])
        scores = jnp.sum(jnp.roll(pieces, index // CORES, axis=0), axis=(0, 1))
    else:
        scores = sum(pieces, local)
    return (scores, gradient)


def solution(mesh):
    placed = (
        P(("group", "expert"), "dp"),
        P(("group", "expert"), None),
        P(("group", "expert"), None),
        P("expert", None, "dp"),
        P(("group", "expert"), "dp", None),
    )
    return jax.shard_map(
        shards,
        mesh=mesh,
        in_specs=placed,
        out_specs=(P(("group", "expert"), None), P(("group", "expert"), None, "dp")),
        check_vma=False,
    )
```

```python
import functools

import jax
import jax.numpy as jnp
from jax import lax
from jax.experimental import pallas as pl
from jax.experimental.pallas import tpu as pltpu
from jax.sharding import PartitionSpec as P

CORES = 2
ROWS = 16
VMEM_LIMIT = 14 * 2**20
VMEM = pl.BlockSpec(memory_space=pltpu.VMEM)
ANY = pl.BlockSpec(memory_space=pl.ANY)


def exchange(value, step):
    count = lax.axis_size("expert")
    return lax.ppermute(value, "expert", [(i, i ^ step) for i in range(count)])


def look_up(table, index):
    return sum(jnp.where(index == i, int(value), 0) for i, value in enumerate(table))


def gather_plan(packed):
    owners = lax.axis_size("expert")
    mine = lax.axis_index("expert")
    own = ([packed], [0] * owners, list(range(owners)))
    if owners != 4:
        return [own] + [
            ([exchange(packed, j)], [0] * owners, [i ^ j for i in range(owners)])
            for j in range(1, owners)
        ]
    send = lambda value, pairs: lax.ppermute(value, "expert", pairs)
    down = send(packed, [(1, 0), (2, 1), (3, 2)])
    up = send(packed, [(0, 1), (1, 2), (2, 3)])
    far = send(packed, [(0, 2), (3, 1)])
    outer = [(1, 0), (2, 3)]
    second = send(jnp.where(mine == 1, down, up), outer)
    third = send(far, outer)
    return [
        own,
        ([down, up], [0, 0, 0, 1], [1, 2, 3, 2]),
        ([second, up], [0, 1, 1, 0], [2, 0, 1, 1]),
        ([third, far], [0, 1, 1, 0], [3, 3, 0, 0]),
    ]


def dp_shift(value, chip_step, core_flip):
    chips = lax.axis_size("dp") // CORES
    pairs = []
    for chip in range(chips):
        for core in range(CORES):
            target = (chip - chip_step) % chips
            pairs.append((chip * CORES + core, target * CORES + (core ^ core_flip)))
    return lax.ppermute(value, "dp", pairs)


def pack(out_grad, routes, route_prob):
    tokens, columns = out_grad.shape
    assert 2 * tokens <= columns and 2 * routes.shape[1] == ROWS
    value = route_prob.T
    high = lax.reduce_precision(value, 8, 7)
    middle = lax.reduce_precision(value - high, 8, 7)
    upper = jnp.concatenate([routes.T.astype(jnp.float32), high], axis=1)
    lower = jnp.concatenate([middle, value - high - middle], axis=1)
    known = jnp.concatenate([upper, lower], axis=0).astype(jnp.bfloat16)
    known = jnp.pad(known, ((0, 0), (0, columns - known.shape[1])))
    return jnp.concatenate([out_grad, known], axis=0)


def saved_at(block, chips):
    index = lax.axis_index("dp")
    chip, core = index // CORES, index % CORES
    return (block % CORES != core) * chips + (block // CORES - chip + chips) % chips


def phase_body(picks, arrays, parts, *refs):
    group = len(picks)
    choices, weight = refs[: sum(arrays)], refs[sum(arrays)]
    routed, keep, send, made, table = refs[-5:]
    experts, rows, columns = routed.shape
    chips = keep.shape[0]
    capacity, share = rows // group, rows // parts
    tokens, fanout = choices[0].shape[0] - ROWS, ROWS // 2
    mine, index = lax.axis_index("expert"), lax.axis_index("dp")
    chip, core = index // CORES, index % CORES

    before = (
        lax.broadcasted_iota(jnp.int32, (tokens, tokens), 0)
        < lax.broadcasted_iota(jnp.int32, (tokens, tokens), 1)
    )
    before = before.astype(jnp.float32).astype(jnp.bfloat16)
    slots = lax.broadcasted_iota(jnp.int32, (capacity, tokens), 0)
    blocks, at = [], 0
    for g in range(group):
        options = choices[at : at + arrays[g]]
        at += arrays[g]
        if len(options) == 1:
            blocks.append(options[0])
            continue
        pick = look_up(picks[g], mine)
        for i, option in enumerate(options):

            @pl.when(pick == i)
            def _(option=option, g=g):
                table[g] = option[...]

        blocks.append(table.at[g])
    for g in range(group):
        known = blocks[g][tokens:, : 2 * tokens].astype(jnp.float32)
        names = known[:fanout, :tokens]
        probs = known[:fanout, tokens:] + known[fanout:, :tokens] + known[fanout:, tokens:]
        named, weights = [], []
        for e in range(experts):
            hit = names == (mine * experts + e).astype(jnp.float32)
            prob = jnp.where(hit, probs, 0.0)
            named.append(jnp.max(hit.astype(jnp.float32), axis=0, keepdims=True))
            weights.append(jnp.sum(prob, axis=0, keepdims=True))
        named = jnp.concatenate(named, axis=0)
        rank = jnp.dot(named.astype(jnp.bfloat16), before, preferred_element_type=jnp.float32)
        place = jnp.where(named > 0.0, rank, -1.0).astype(jnp.int32)
        for e in range(experts):
            taken = slots == place[e : e + 1, :]
            chosen = jnp.dot(
                taken.astype(jnp.float32).astype(jnp.bfloat16),
                blocks[g][:tokens],
                preferred_element_type=jnp.float32,
            )
            scale = jnp.sum(jnp.where(taken, weights[e], 0.0), axis=1, keepdims=True)
            routed[e, g * capacity : (g + 1) * capacity, :] = (chosen * scale).astype(jnp.bfloat16)
    for e in range(experts):
        value = lax.dot_general(
            weight[e], routed[e], (((1,), (1,)), ((), ())), preferred_element_type=jnp.float32
        )
        value = value.T.astype(jnp.bfloat16)
        for p in range(parts):
            made[e * parts + p] = value[p * share : (p + 1) * share]
    for k in range(chips):
        near = (chip + k) % chips * CORES
        keep[k] = made[near + core]
        send[k] = made[near + 1 - core]


def phase(blocks, down_weight, capacity, parts, after):
    experts, hidden, columns = down_weight.shape
    group = len(blocks)
    arrays = [len(options) for options, _, _ in blocks]
    flat = [array for options, _, _ in blocks for array in options]
    rows = group * capacity
    chips = experts * parts // CORES
    half = jax.ShapeDtypeStruct((chips, rows // parts, hidden), jnp.bfloat16)
    return pl.pallas_call(
        functools.partial(phase_body, [pick for _, pick, _ in blocks], arrays, parts),
        in_specs=[VMEM] * (len(flat) + 1) + [ANY] * len(after),
        out_specs=[VMEM] * 3,
        out_shape=[jax.ShapeDtypeStruct((experts, rows, columns), jnp.bfloat16), half, half],
        scratch_shapes=[
            pltpu.VMEM((experts * parts, rows // parts, hidden), jnp.bfloat16),
            pltpu.VMEM((group,) + flat[0].shape, jnp.bfloat16),
        ],
        compiler_params=pltpu.CompilerParams(vmem_limit_bytes=VMEM_LIMIT),
        cost_estimate=pl.CostEstimate(
            flops=5 * experts * rows * columns * hidden,
            bytes_accessed=5 * experts * hidden * columns,
            transcendentals=0,
        ),
    )(*flat, down_weight, *after)


def copy_expert(first, second, expert, target):
    early = first.shape[0]

    @pl.when(expert < early)
    def _():
        target[...] = first[jnp.minimum(expert, early - 1)]

    @pl.when(expert >= early)
    def _():
        target[...] = second[jnp.maximum(expert - early, 0)]


def score_body(tables, pieces, parts, *refs):
    out, table = refs[-2:]
    spread, capacity, _ = table.shape
    first, second = refs[:spread], refs[spread : 2 * spread]
    hidden = refs[2 * spread : 2 * spread + pieces]
    phases = pieces * CORES // spread
    group, per = len(tables) // phases, spread // CORES
    chips = spread // CORES
    mine, index = lax.axis_index("expert"), lax.axis_index("dp")
    expert = index // parts
    row = index % parts * hidden[0].shape[0]
    for i in range(spread):
        copy_expert(first[i], second[i], expert, table.at[i])
    total = jnp.zeros((1, out.shape[1]), jnp.float32)
    for j in range(phases):
        grad = hidden[j * per][...]
        for more in hidden[j * per + 1 : (j + 1) * per]:
            grad = grad + more[...].astype(jnp.float32)
        block = sum(
            jnp.where(row // capacity == g, look_up(tables[j * group + g], mine), 0)
            for g in range(group)
        )
        at = saved_at(block, chips)
        offset = pl.multiple_of(row % capacity, ROWS)
        kept = table[at, pl.ds(offset, grad.shape[0]), :].astype(jnp.float32)
        total = total + jnp.sum((kept * grad) ** 2, axis=0, keepdims=True)
    line = lax.broadcasted_iota(jnp.int32, out.shape, 0)
    out[...] = jnp.where(line == expert, total, 0.0)


def score(saved, hidden, tables, parts, after):
    spread = len(saved) // 2
    _, share, width = saved[0].shape
    experts = saved[0].shape[0] + saved[spread].shape[0]
    flat = [piece for pieces in hidden for piece in pieces]
    return pl.pallas_call(
        functools.partial(score_body, tables, len(flat), parts),
        in_specs=[VMEM] * (len(saved) + len(flat)) + [ANY] * len(after),
        out_specs=VMEM,
        out_shape=jax.ShapeDtypeStruct((experts, width), jnp.float32),
        scratch_shapes=[pltpu.VMEM((spread, share, width), jnp.bfloat16)],
        compiler_params=pltpu.CompilerParams(vmem_limit_bytes=VMEM_LIMIT),
    )(*saved, *flat, *after)


def gradient_body(spread, tables, *refs):
    first, second, routed = refs[:spread], refs[spread : 2 * spread], refs[2 * spread : -3]
    out, done, rows = refs[-3:]
    done[...] = jnp.zeros_like(done)
    e = pl.program_id(0)
    share = first[0].shape[1]
    mine, index = lax.axis_index("expert"), lax.axis_index("dp")
    chips = spread // CORES
    for i in range(spread):
        near = (index // CORES + i % chips) % chips * CORES
        block = near + (index % CORES if i < chips else 1 - index % CORES)
        order = sum(
            jnp.where(look_up(table, mine) == block, j, 0) for j, table in enumerate(tables)
        )
        at = pl.multiple_of(order * share, share)
        copy_expert(first[i], second[i], e, rows.at[pl.ds(at, share)])
    whole = jnp.concatenate([part[e] for part in routed], axis=0)
    out[0] = lax.dot_general(
        rows[...], whole, (((0,), (0,)), ((), ())), preferred_element_type=jnp.float32
    ).astype(jnp.bfloat16)


def gradient_of(saved, routed, tables):
    spread = len(saved) // 2
    _, share, hidden = saved[0].shape
    experts, _, columns = routed[0].shape
    slots = share * spread
    return pl.pallas_call(
        functools.partial(gradient_body, spread, tables),
        grid=(experts,),
        in_specs=[VMEM] * (len(saved) + len(routed)),
        out_specs=[
            pl.BlockSpec((1, hidden, columns), lambda e: (e, 0, 0)),
            pl.BlockSpec((8, 128), lambda e: (0, 0)),
        ],
        out_shape=[
            jax.ShapeDtypeStruct((experts, hidden, columns), jnp.bfloat16),
            jax.ShapeDtypeStruct((8, 128), jnp.float32),
        ],
        scratch_shapes=[pltpu.VMEM((slots, hidden), jnp.bfloat16)],
        compiler_params=pltpu.CompilerParams(vmem_limit_bytes=VMEM_LIMIT),
        cost_estimate=pl.CostEstimate(
            flops=5 * experts * slots * columns * hidden,
            bytes_accessed=5 * experts * hidden * columns,
            transcendentals=0,
        ),
    )(*saved, *routed)


def shards(out_grad, routes, route_prob, down_weight, saved_hidden):
    owners = lax.axis_size("expert")
    dp_count = lax.axis_size("dp")
    chips = dp_count // CORES
    experts, capacity, _ = saved_hidden.shape
    assert owners == dp_count and dp_count % experts == 0
    parts = dp_count // experts
    group = max(1, parts * ROWS // capacity)
    phases = owners // group
    index = lax.axis_index("dp")

    packed = pack(out_grad, routes, route_prob)
    plan = gather_plan(packed)
    tables = [table for _, _, table in plan]

    halves = [saved_hidden[: experts // 2], saved_hidden[experts // 2 :]]
    halves = [
        [half] + [dp_shift(half, step, 0) for step in range(1, chips)] for half in halves
    ]

    routed, hidden = [None] * phases, [None] * phases
    for j in range(phases):
        routed[j], keep, send = phase(
            plan[j * group : (j + 1) * group],
            down_weight,
            capacity,
            parts,
            halves[0][1:]
            if j == 0
            else hidden[0][:1]
            if j == 2
            else hidden[0][1:] + hidden[1][:1]
            if j == 3
            else [],
        )
        other = dp_shift(send, 0, 1)
        total = keep.astype(jnp.float32) + other.astype(jnp.float32)
        hidden[j] = [total[0]] + [
            dp_shift(total[step].astype(jnp.bfloat16), -step, 0) for step in range(1, chips)
        ]
    halves = [half + [dp_shift(part, 0, 1) for part in half] for half in halves]
    saved = halves[0] + halves[1]
    gradient, done = gradient_of(saved, routed, tables)
    local = score(saved, hidden, tables, parts, [done])
    pieces = [
        dp_shift(local, step, flip)
        for step in range(chips)
        for flip in range(CORES)
        if step + flip
    ]
    if parts > 1:
        pieces = jnp.stack([local] + pieces).reshape(chips, CORES, experts, -1)
        pieces = jnp.where(index % CORES == 0, pieces, pieces[:, ::-1])
        scores = jnp.sum(jnp.roll(pieces, index // CORES, axis=0), axis=(0, 1))
    else:
        scores = sum(pieces, local)
    return (scores, gradient)


def solution(mesh):
    placed = (
        P(("group", "expert"), "dp"),
        P(("group", "expert"), None),
        P(("group", "expert"), None),
        P("expert", None, "dp"),
        P(("group", "expert"), "dp", None),
    )
    return jax.shard_map(
        shards,
        mesh=mesh,
        in_specs=placed,
        out_specs=(P(("group", "expert"), None), P(("group", "expert"), None, "dp")),
        check_vma=False,
    )
```
